512 devices in a mesh: frame: 16 (over z_hi, x), space: 32 (over z_lo, y, core).
Axes of the slice: x: 4, y: 8, z: 8 (z_hi: 4, z_lo: 2; z = z_hi * 2 + z_lo), core: 2. Of those that a mesh axis runs over, the one named last changes fastest.
Arguments:
- qkv_now: bfloat16 [4096, 16, 384], P('space', 'frame'), as said below
- past_cache: bfloat16 [16, 4096, 16, 256], P('frame', 'space'), may hold values from -6 to 6
- frame_rank: int32 [16], replicated, may hold values from 0 to 15, each once
- frame_depth: int32 [32], replicated, may hold values from 0 to 16, as said below
- tile_lists: int32 [32, 32], replicated, may hold values from 0 to 1, as said below
Outputs:
- attended: bfloat16 [4096, 2048], P('space', 'frame')
The draws below stay inside these ranges and needn't reach their ends.
Inputs may be any that keep to these rules, and one draw needn't show every extreme that they name: Entries of qkv_now lie within -5 to 5. `frame_depth`: some tile sees every past frame. `tile_lists`: entry [t, u] is 1 exactly where the distance between tiles t and u around the closed loop of 32 tiles is at most a radius of tile t; the diagonal is 1 and some tile sees all tiles.
All inputs are finite; a program needn't handle non-finite values.
Results may differ from the reference program's by a relative error of at most 0.01.
Values may be sent and summed in bfloat16 or wider, within the bound.
No kernel may reach another device: no remote copies, remote signals or barrier semaphores. Data moves between devices by JAX's collectives and lax.ppermute only.
A program may use at most 64 MiB of HBM per device.

```python
import math
import jax
import jax.numpy as jnp
from jax import lax

HEADS = 16
HEAD_DIM = 128
TOK_DEV = 128
TILES = 32
CUR_TOK = 4096
PAST = 16


def draw_qkv_now(key, part):
    key = jax.random.fold_in(key, 11)
    first = jax.random.fold_in(key, 0)
    shape = (CUR_TOK, HEADS, 3 * HEAD_DIM)
    values = jax.random.truncated_normal(first, -5.0, 5.0, shape, jnp.float32)
    return values.astype(jnp.bfloat16)


def draw_frame_depth(key, part):
    key = jax.random.fold_in(key, 13)
    first, second = jax.random.split(key)
    depth = jax.random.randint(first, (TILES,), 0, PAST + 1, dtype=jnp.int32)
    chosen = jax.random.randint(second, (), 0, TILES, dtype=jnp.int32)
    return jnp.where(jnp.arange(TILES, dtype=jnp.int32) == chosen, PAST, depth).astype(jnp.int32)


def draw_tile_lists(key, part):
    key = jax.random.fold_in(key, 12)
    first, second = jax.random.split(key)
    radius = jax.random.randint(first, (TILES,), 0, TILES // 2 + 1, dtype=jnp.int32)
    chosen = jax.random.randint(second, (), 0, TILES, dtype=jnp.int32)
    indices = jnp.arange(TILES, dtype=jnp.int32)
    radius = jnp.where(indices == chosen, TILES // 2, radius)
    apart = jnp.abs(indices[:, None] - indices[None, :])
    beside_all = jnp.minimum(apart, TILES - apart)
    return (beside_all <= radius[:, None]).astype(jnp.int32)


def steps_of(key, shape, cuts, low, top_value):
    factor_of = 1.0
    for axis_at, shards_of in cuts:
        steps = jax.random.uniform(jax.random.fold_in(jax.random.fold_in(key, 6), axis_at), (shards_of,), jnp.float32, low / len(cuts), top_value / len(cuts))
        factor_of = factor_of * jnp.repeat(jnp.exp(steps), shape[axis_at] // shards_of).reshape((-1,) + (1,) * (len(shape) - 1 - axis_at))
    return factor_of


def normal_values(own_key, shape, deviation, limit, shards=(), kind=jnp.bfloat16):
    level = steps_of(own_key, shape, shards, -0.22, 0.18) if shards else 1.0
    values = jax.random.normal(own_key, shape, jnp.float32) * deviation * level
    return jnp.minimum(jnp.maximum(values, -limit), limit).astype(kind)


def setup_inputs(seed: int = 0) -> dict:
    seeds = jax.random.split(jax.random.key(seed), 6)
    qkv_now = draw_qkv_now(jax.random.fold_in(seeds[5], 71), 0)
    past_cache = normal_values(seeds[1], (PAST, CUR_TOK, HEADS, 2 * HEAD_DIM), 1.0, 6.0, ((0, 16), (1, 32)))
    frame_rank = jax.random.permutation(seeds[2], PAST).astype(jnp.int32)
    frame_depth = draw_frame_depth(jax.random.fold_in(seeds[5], 71), 0)
    tile_lists = draw_tile_lists(jax.random.fold_in(seeds[5], 71), 0)
    return {"qkv_now": qkv_now, "past_cache": past_cache, "frame_rank": frame_rank, "frame_depth": frame_depth, "tile_lists": tile_lists}


NEG = -1e+30

def reference(qkv_now, past_cache, frame_rank, frame_depth, tile_lists):
    score_scale = 1.0 / math.sqrt(HEAD_DIM)
    group_len = (PAST + 1) * TOK_DEV
    frame_seen = (frame_rank[None, :] >= PAST - frame_depth[:, None]).astype(jnp.float32)

    def one_tile(tile):
        queries = lax.dynamic_slice_in_dim(qkv_now, (tile * TOK_DEV).astype(jnp.int32), TOK_DEV, 0)
        row_list = lax.dynamic_index_in_dim(tile_lists, tile, 0, False).astype(jnp.float32)
        seen = lax.dynamic_index_in_dim(frame_seen, tile, 0, False)
        group_seen = jnp.concatenate([seen, jnp.ones((1,), jnp.float32)])
        visible = jnp.broadcast_to(row_list[:, None, None] * group_seen[None, :, None], (TILES, PAST + 1, TOK_DEV)).reshape(TILES, group_len)

        def one_head(head):
            query = lax.dynamic_index_in_dim(queries, head, 1, False)[:, :HEAD_DIM].astype(jnp.float32)
            current = lax.dynamic_index_in_dim(qkv_now, head, 1, False)[:, HEAD_DIM:].reshape(TILES, 1, TOK_DEV, 2 * HEAD_DIM)
            cached = lax.dynamic_index_in_dim(past_cache, head, 2, False).reshape(PAST, TILES, TOK_DEV, 2 * HEAD_DIM).transpose(1, 0, 2, 3)
            grouped = jnp.concatenate([cached, current], 1).reshape(TILES, group_len, 2 * HEAD_DIM).astype(jnp.float32)
            scores = jnp.einsum('qd,ugd->qug', query, grouped[..., :HEAD_DIM], precision=lax.Precision.HIGHEST) * score_scale
            masked = jnp.where(visible[None] > 0, scores, NEG)
            peak = lax.optimization_barrier(jnp.max(masked, axis=2))
            weights = jnp.exp(masked - peak[..., None]) * visible[None]
            totals = lax.optimization_barrier(jnp.sum(weights, axis=2))
            rounded = weights.astype(jnp.bfloat16).astype(jnp.float32)
            weighted = jnp.einsum('qug,ugd->qud', rounded, grouped[..., HEAD_DIM:], precision=lax.Precision.HIGHEST)
            safe = jnp.maximum(totals, 1.0)
            share = (weighted / safe[..., None]).astype(jnp.bfloat16).astype(jnp.float32)
            lse = peak + jnp.log(safe)
            top = lax.optimization_barrier(jnp.max(lse, axis=1, keepdims=True))
            factor = jnp.exp(lse - top)
            return lax.optimization_barrier(jnp.sum(share * factor[..., None], axis=1)) / lax.optimization_barrier(jnp.sum(factor, axis=1))[:, None]
        return lax.map(one_head, jnp.arange(HEADS, dtype=jnp.int32))
    result = lax.map(one_tile, jnp.arange(TILES, dtype=jnp.int32))
    return result.transpose(0, 2, 1, 3).reshape(CUR_TOK, HEADS * HEAD_DIM).astype(jnp.bfloat16)
```

```python
import functools
import math

import jax
import jax.numpy as jnp
from jax import lax
from jax.experimental import pallas as pl
from jax.experimental.pallas import tpu as pltpu
from jax.sharding import PartitionSpec as P

NEG = -1e30
LSE_ROWS = 16


def slot_buckets(slots):
    sizes = [size for size in (2, 4, 6, 9, 13) if size < slots]
    return sizes + [slots]


def attend_kernel(
    scale, table, q_ref, past_own, now_own, past_other, now_other, out_ref, keys, values, scores, probs, lse_cols
):
    tiles, tok, size = q_ref.shape
    slots = past_own.shape[0] + 1
    width = 2 * tok
    ones = jnp.ones((tok, size), jnp.bfloat16)
    for slot in range(slots):
        for which, (past, now) in enumerate(((past_own, now_own), (past_other, now_other))):
            block = now[...] if slot == 0 else past[table[slot - 1]]
            first = (2 * slot + which) * tok
            keys[first : first + tok, :] = block[:, :size]
            values[first : first + tok, :size] = block[:, size:]
            values[first : first + tok, size:] = ones
    lse_cols[...] = jnp.full(lse_cols.shape, NEG, jnp.float32)
    lanes = lax.broadcasted_iota(jnp.int32, (tok, tok), 1)
    buckets = slot_buckets(slots)

    def one_pair(pair, _):
        base = slots - 1 + pair * 8
        tile_a, tile_b = table[base], table[base + 1]
        place_a, place_b = table[base + 2], table[base + 3]
        limits = ((table[base + 4], table[base + 5]), (table[base + 6], table[base + 7]))
        most = jnp.maximum(
            jnp.maximum(limits[0][0], limits[0][1]), jnp.maximum(limits[1][0], limits[1][1])
        )

        @pl.when(most == 0)
        def _():
            out_ref[tile_a, :tok, :] = jnp.zeros((tok, size), jnp.bfloat16)
            out_ref[tile_b, :tok, :] = jnp.zeros((tok, size), jnp.bfloat16)

        def work(count):
            queries = jnp.concatenate([q_ref[place_a], q_ref[place_b]], 0)
            peak = None
            for slot in range(count):
                cut = slice(slot * width, (slot + 1) * width)
                raw = lax.dot_general(
                    queries, keys[cut, :], (((1,), (1,)), ((), ())), preferred_element_type=jnp.float32
                )
                rows = []
                for half in range(2):
                    row = []
                    for which in range(2):
                        block = raw[half * tok : (half + 1) * tok, which * tok : (which + 1) * tok]
                        shift = jnp.where(slot < limits[half][which], 0.0, NEG)
                        row.append(block + shift)
                    rows.append(row)
                for half in range(2):
                    for which in range(2):
                        scores[
                            half * tok : (half + 1) * tok,
                            slot * width + which * tok : slot * width + (which + 1) * tok,
                        ] = rows[half][which]
                best = jnp.concatenate([jnp.maximum(row[0], row[1]) for row in rows], 0)
                peak = best if peak is None else jnp.maximum(peak, best)
            peak = jnp.max(peak, axis=1, keepdims=True)
            for slot in range(count):
                cut = slice(slot * width, (slot + 1) * width)
                probs[:, cut] = jnp.exp2(
                    (scores[:, cut] - peak) * (scale * math.log2(math.e))
                ).astype(jnp.bfloat16)
            summed = jnp.dot(
                probs[:, : count * width], values[: count * width, :], preferred_element_type=jnp.float32
            )
            total = summed[:, size:]
            share = (summed[:, :size] / total).astype(jnp.bfloat16)
            out_ref[tile_a, :tok, :] = share[:tok]
            out_ref[tile_b, :tok, :] = share[tok:]
            lse = peak * scale + jnp.log(total)
            cols = jnp.where(lanes == tile_a, lse[:tok], lse_cols[...])
            lse_cols[...] = jnp.where(lanes == tile_b, lse[tok:], cols)

        low = 0
        for count in buckets:
            pl.when((most > low) & (most <= count))(functools.partial(work, count))
            low = count
        return 0

    lax.fori_loop(0, tiles // 2, one_pair, 0)
    lse = lse_cols[...].T[:tiles]
    high = lse.astype(jnp.bfloat16).astype(jnp.float32)
    rest = lse - high
    middle = rest.astype(jnp.bfloat16).astype(jnp.float32)
    low_part = rest - middle
    row_ids = lax.broadcasted_iota(jnp.int32, (LSE_ROWS, tok), 0)
    for tile in range(tiles):
        rows = jnp.where(row_ids == 0, high[tile : tile + 1], 0.0)
        rows = jnp.where(row_ids == 1, middle[tile : tile + 1], rows)
        rows = jnp.where(row_ids == 2, low_part[tile : tile + 1], rows)
        out_ref[tile, tok : tok + LSE_ROWS, :] = rows.astype(jnp.bfloat16)


def combine_kernel(in_ref, out_ref):
    tiles = in_ref.shape[0]
    tok, size = out_ref.shape
    lse = jnp.concatenate(
        [
            jnp.sum(in_ref[tile, tok : tok + LSE_ROWS, :].astype(jnp.float32), axis=0, keepdims=True)
            for tile in range(tiles)
        ],
        0,
    )
    factor = jnp.exp(lse - jnp.max(lse, axis=0, keepdims=True))
    factor = factor / jnp.sum(factor, axis=0, keepdims=True)
    if tiles < tok:
        factor = jnp.concatenate([factor, jnp.zeros((tok - tiles, tok), jnp.float32)], 0)
    factor = factor.T
    total = jnp.zeros((tok, size), jnp.float32)
    for tile in range(tiles):
        total += in_ref[tile, :tok, :].astype(jnp.float32) * factor[:, tile : tile + 1]
    out_ref[...] = total.astype(jnp.bfloat16)


def work_table(frame_rank, frame_depth, tile_lists, position, core, tiles, frames):
    ids = jnp.arange(frames, dtype=jnp.int32)
    by_rank = jnp.sum(
        jnp.where(frame_rank[None, :] == (frames - 1 - ids)[:, None], ids[None, :], 0), axis=1
    )
    own = 2 * position + core
    mine = tile_lists.reshape(tiles, 2, 2 * tiles)
    mine = lax.dynamic_index_in_dim(mine, core, 1, False)
    sees_own = lax.dynamic_index_in_dim(mine, own, 1, False)
    sees_other = lax.dynamic_index_in_dim(mine, own + 1 - 2 * core, 1, False)
    depth = lax.dynamic_index_in_dim(frame_depth.reshape(tiles, 2), core, 1, False) + 1
    own_slots = jnp.where(sees_own == 1, depth, 0)
    other_slots = jnp.where(sees_other == 1, depth, 0)
    most = jnp.maximum(own_slots, other_slots)
    tile_ids = jnp.arange(tiles, dtype=jnp.int32)
    before = (most[None, :] > most[:, None]) | (
        (most[None, :] == most[:, None]) & (tile_ids[None, :] < tile_ids[:, None])
    )
    rank = jnp.sum(before.astype(jnp.int32), axis=1)
    chosen = rank[None, :] == tile_ids[:, None]

    def ordered(values):
        return jnp.sum(jnp.where(chosen, values[None, :], 0), axis=1)

    tile = ordered(tile_ids)
    place = ordered(tile_ids ^ position)
    first, second = ordered(own_slots), ordered(other_slots)
    pairs = jnp.stack([tile, place, first, second], 1).reshape(tiles // 2, 2, 4)
    pairs = jnp.concatenate(
        [pairs[:, :, 0], pairs[:, :, 1], pairs[:, 0, 2:], pairs[:, 1, 2:]], axis=1
    ).reshape(-1)
    return jnp.concatenate([by_rank, pairs]).astype(jnp.int32)


def body(qkv_now, past_cache, frame_rank, frame_depth, tile_lists):
    tok = qkv_now.shape[0]
    size = qkv_now.shape[2] // 3
    space = lax.axis_size("space")
    frames = lax.axis_size("frame")
    tiles = space // 2
    index = lax.axis_index("space")
    position, core = index // 2, index % 2
    scale = 1.0 / math.sqrt(size)

    def swap(array, bit):
        return lax.ppermute(array, "space", [(i, i ^ bit) for i in range(space)])

    by_head = past_cache[0].transpose(1, 0, 2)
    past_own = lax.all_to_all(by_head, "frame", split_axis=0, concat_axis=0, tiled=True)

    now = qkv_now[:, 0, :]
    queries = now[None, :, :size]
    bit = 2
    while bit < space:
        queries = jnp.concatenate([queries, swap(queries, bit)], 0)
        bit *= 2
    now_own = now[:, size:]
    now_other = swap(now_own, 1)
    table = work_table(frame_rank, frame_depth, tile_lists, position, core, tiles, frames)

    past_other = swap(past_own, 1)
    slots = frames + 1
    vmem = pl.BlockSpec(memory_space=pltpu.VMEM)
    partial = pl.pallas_call(
        functools.partial(attend_kernel, scale),
        out_shape=jax.ShapeDtypeStruct((tiles, tok + LSE_ROWS, size), jnp.bfloat16),
        in_specs=[pl.BlockSpec(memory_space=pltpu.SMEM)] + [vmem] * 5,
        out_specs=vmem,
        scratch_shapes=[
            pltpu.VMEM((2 * slots * tok, size), jnp.bfloat16),
            pltpu.VMEM((2 * slots * tok, 2 * size), jnp.bfloat16),
            pltpu.VMEM((2 * tok, 2 * slots * tok), jnp.float32),
            pltpu.VMEM((2 * tok, 2 * slots * tok), jnp.bfloat16),
            pltpu.VMEM((tok, tok), jnp.float32),
        ],
        compiler_params=pltpu.CompilerParams(vmem_limit_bytes=40 * 2**20),
        name="attend",
    )(table, queries, past_own, now_own, past_other, now_other)

    groups = [[2 * place + which for place in range(tiles)] for which in range(2)]
    received = lax.all_to_all(
        partial, "space", split_axis=0, concat_axis=0, axis_index_groups=groups, tiled=True
    )
    return pl.pallas_call(
        combine_kernel,
        out_shape=jax.ShapeDtypeStruct((tok, size), jnp.bfloat16),
        in_specs=[vmem],
        out_specs=vmem,
        name="combine",
    )(received)


def solution(mesh):
    in_specs = (P("space", "frame", None), P("frame", "space", None, None), P(), P(), P())
    out_specs = P("space", "frame")
    return jax.shard_map(body, mesh=mesh, in_specs=in_specs, out_specs=out_specs, check_vma=False)
```

```python
import functools
import math

import jax
import jax.numpy as jnp
from jax import lax
from jax.experimental import pallas as pl
from jax.experimental.pallas import tpu as pltpu
from jax.sharding import PartitionSpec as P

NEG = -1e30
LSE_ROWS = 16
GROUP = 4


def slot_buckets(slots):
    sizes = [size for size in (1, 2, 3, 4, 5, 6, 7, 8, 9, 11, 13, 15) if size < slots]
    return sizes + [slots]


def attend_kernel(
    scale, table, q_ref, past_own, now_own, past_other, now_other, out_ref, values, scores
):
    tiles, tok, size = q_ref.shape
    slots = past_own.shape[0] + 1
    sources = ((past_own, now_own), (past_other, now_other))

    def block_of(slot, which):
        past, now = sources[which]
        return now[...] if slot == 0 else past[table[slot - 1]]

    def first_of(slot, which):
        return (2 * slot + which) * tok

    for slot in range(slots):
        for which in range(2):
            first = first_of(slot, which)
            values[:size, first : first + tok] = block_of(slot, which)[:, size:].T
    values[size:, :] = jnp.ones((LSE_ROWS, 2 * slots * tok), jnp.bfloat16)
    row_ids = lax.broadcasted_iota(jnp.int32, (LSE_ROWS, tok), 0)
    buckets = slot_buckets(slots)

    def one_group(group, _):
        base = slots - 1 + group * (4 * GROUP)
        group_tiles = [table[base + member * 4] for member in range(GROUP)]
        places = [table[base + member * 4 + 1] for member in range(GROUP)]
        limits = [(table[base + member * 4 + 2], table[base + member * 4 + 3]) for member in range(GROUP)]
        most = functools.reduce(jnp.maximum, [limit for both in limits for limit in both])

        @pl.when(most == 0)
        def _():
            for tile in group_tiles:
                out_ref[tile, :size, :] = jnp.zeros((size, tok), jnp.bfloat16)
                out_ref[tile, size:, :] = jnp.where(row_ids == 0, NEG, 0.0).astype(jnp.bfloat16)

        def work(count):
            queries = jnp.concatenate([q_ref[place].T for place in places], 1)
            peaks = [jnp.full((8, tok), NEG, jnp.float32) for _ in range(GROUP)]
            for slot in range(count):
                for which in range(2):
                    first = first_of(slot, which)
                    raw = jnp.dot(
                        block_of(slot, which)[:, :size], queries, preferred_element_type=jnp.float32
                    )
                    scores[first : first + tok, :] = raw
                    for half in range(GROUP):
                        best = jnp.max(
                            raw[:, half * tok : (half + 1) * tok].reshape(tok // 8, 8, tok), axis=0
                        )
                        best = jnp.where(slot < limits[half][which], best, NEG)
                        peaks[half] = jnp.maximum(peaks[half], best)
            peaks = [jnp.max(peak, axis=0, keepdims=True) for peak in peaks]
            summed = None
            for slot in range(count):
                chunk = []
                for which in range(2):
                    first = first_of(slot, which)
                    shift = jnp.concatenate(
                        [jnp.where(slot < limits[half][which], peaks[half], -NEG) for half in range(GROUP)],
                        1,
                    )
                    chunk.append(
                        jnp.exp2(
                            (scores[first : first + tok, :] - shift) * (scale * math.log2(math.e))
                        ).astype(jnp.bfloat16)
                    )
                start = first_of(slot, 0)
                term = jnp.dot(
                    values[:, start : start + 2 * tok],
                    jnp.concatenate(chunk, 0),
                    preferred_element_type=jnp.float32,
                )
                summed = term if summed is None else summed + term
            total = jnp.maximum(summed[size : size + 1, :], 1.0)
            share = (summed[:size, :] / total).astype(jnp.bfloat16)
            lse = jnp.concatenate(peaks, 1) * scale + jnp.log(total)
            high = lse.astype(jnp.bfloat16).astype(jnp.float32)
            rest = lse - high
            middle = rest.astype(jnp.bfloat16).astype(jnp.float32)
            low_part = rest - middle
            for half, tile in enumerate(group_tiles):
                cut = slice(half * tok, (half + 1) * tok)
                rows = jnp.where(row_ids == 0, high[:, cut], 0.0)
                rows = jnp.where(row_ids == 1, middle[:, cut], rows)
                rows = jnp.where(row_ids == 2, low_part[:, cut], rows)
                out_ref[tile, :size, :] = share[:, cut]
                out_ref[tile, size:, :] = rows.astype(jnp.bfloat16)

        low = 0
        for count in buckets:
            pl.when((most > low) & (most <= count))(functools.partial(work, count))
            low = count
        return 0

    lax.fori_loop(0, tiles // GROUP, one_group, 0)


def attend_call(scale, table, queries, past_own, now_own, past_other, now_other):
    tiles, tok, size = queries.shape
    slots = past_own.shape[0] + 1
    vmem = pl.BlockSpec(memory_space=pltpu.VMEM)
    return pl.pallas_call(
        functools.partial(attend_kernel, scale),
        out_shape=jax.ShapeDtypeStruct((tiles, size + LSE_ROWS, tok), jnp.bfloat16),
        in_specs=[pl.BlockSpec(memory_space=pltpu.SMEM)] + [vmem] * 5,
        out_specs=vmem,
        scratch_shapes=[
            pltpu.VMEM((size + LSE_ROWS, 2 * slots * tok), jnp.bfloat16),
            pltpu.VMEM((2 * slots * tok, GROUP * tok), jnp.float32),
        ],
        compiler_params=pltpu.CompilerParams(vmem_limit_bytes=40 * 2**20),
        name="attend",
    )(table, queries, past_own, now_own, past_other, now_other)


def combine_kernel(in_ref, out_ref):
    tiles = in_ref.shape[0]
    tok, size = out_ref.shape
    lse = jnp.concatenate(
        [
            jnp.sum(in_ref[tile, size:, :].astype(jnp.float32), axis=0, keepdims=True)
            for tile in range(tiles)
        ],
        0,
    )
    factor = jnp.exp(lse - jnp.max(lse, axis=0, keepdims=True))
    factor = factor / jnp.sum(factor, axis=0, keepdims=True)
    total = in_ref[0, :size, :].astype(jnp.float32) * factor[0:1]
    for tile in range(1, tiles):
        total += in_ref[tile, :size, :].astype(jnp.float32) * factor[tile : tile + 1]
    out_ref[...] = total.T.astype(jnp.bfloat16)


def gather_bits(tiles):
    bits = [1 << k for k in range(tiles.bit_length() - 1)]
    return [bits[2], bits[1], bits[0], bits[3]] if len(bits) == 4 else bits[::-1]


def work_table(frame_rank, frame_depth, tile_lists, position, core, tiles, frames):
    ids = jnp.arange(frames, dtype=jnp.int32)
    by_rank = jnp.sum(
        jnp.where(frame_rank[None, :] == (frames - 1 - ids)[:, None], ids[None, :], 0), axis=1
    )
    own = 2 * position + core
    mine = tile_lists.reshape(tiles, 2, 2 * tiles)
    mine = lax.dynamic_index_in_dim(mine, core, 1, False)
    sees_own = lax.dynamic_index_in_dim(mine, own, 1, False)
    sees_other = lax.dynamic_index_in_dim(mine, own + 1 - 2 * core, 1, False)
    depth = lax.dynamic_index_in_dim(frame_depth.reshape(tiles, 2), core, 1, False) + 1
    own_slots = jnp.where(sees_own == 1, depth, 0)
    other_slots = jnp.where(sees_other == 1, depth, 0)
    most = jnp.maximum(own_slots, other_slots)
    tile_ids = jnp.arange(tiles, dtype=jnp.int32)
    before = (most[None, :] > most[:, None]) | (
        (most[None, :] == most[:, None]) & (tile_ids[None, :] < tile_ids[:, None])
    )
    rank = jnp.sum(before.astype(jnp.int32), axis=1)
    chosen = rank[None, :] == tile_ids[:, None]

    def ordered(values):
        return jnp.sum(jnp.where(chosen, values[None, :], 0), axis=1)

    tile = ordered(tile_ids)
    apart = tile_ids ^ position
    place = jnp.zeros_like(tile_ids)
    for k, bit in enumerate(gather_bits(tiles)):
        place = place + jnp.where((apart & bit) != 0, 1 << k, 0)
    place = ordered(place)
    first, second = ordered(own_slots), ordered(other_slots)
    pairs = jnp.stack([tile, place, first, second], 1).reshape(-1)
    return jnp.concatenate([by_rank, pairs]).astype(jnp.int32)


def body(qkv_now, past_cache, frame_rank, frame_depth, tile_lists):
    tok = qkv_now.shape[0]
    size = qkv_now.shape[2] // 3
    space = lax.axis_size("space")
    frames = lax.axis_size("frame")
    tiles = space // 2
    index = lax.axis_index("space")
    position, core = index // 2, index % 2
    scale = 1.0 / math.sqrt(size)

    def swap(array, bit):
        return lax.ppermute(array, "space", [(i, i ^ bit) for i in range(space)])

    by_head = past_cache[0].transpose(1, 0, 2)
    past_own = lax.all_to_all(by_head, "frame", split_axis=0, concat_axis=0, tiled=True)

    now = qkv_now[:, 0, :]
    queries = now[None, :, :size]
    for bit in gather_bits(tiles):
        queries = jnp.concatenate([queries, swap(queries, 2 * bit)], 0)
    now_own = now[:, size:]
    now_other = swap(now_own, 1)
    table = work_table(frame_rank, frame_depth, tile_lists, position, core, tiles, frames)

    past_own, queries = lax.optimization_barrier((past_own, queries))
    past_other = swap(past_own, 1)
    partial = attend_call(scale, table, queries, past_own, now_own, past_other, now_other)
    groups = [[2 * place + which for place in range(tiles)] for which in range(2)]
    received = lax.all_to_all(
        partial, "space", split_axis=0, concat_axis=0, axis_index_groups=groups, tiled=True
    )
    return pl.pallas_call(
        combine_kernel,
        out_shape=jax.ShapeDtypeStruct((tok, size), jnp.bfloat16),
        name="combine",
    )(received)


def solution(mesh):
    in_specs = (P("space", "frame", None), P("frame", "space", None, None), P(), P(), P())
    out_specs = P("space", "frame")
    return jax.shard_map(body, mesh=mesh, in_specs=in_specs, out_specs=out_specs, check_vma=False)
```

```python
import functools
import math

import jax
import jax.numpy as jnp
from jax import lax
from jax.experimental import pallas as pl
from jax.experimental.pallas import tpu as pltpu
from jax.sharding import PartitionSpec as P

NEG = -1e30
LSE_ROWS = 16
GROUP = 4


def slot_buckets(slots):
    sizes = [size for size in (1, 2, 3, 4, 5, 6, 7, 8, 9, 11, 13, 15) if size < slots]
    return sizes + [slots]


def attend_kernel(scale, merge, *refs):
    if merge:
        table, queries, past, now, near_part, far_part, out_ref, values, scores = refs
    else:
        table, queries, past, now, out_ref, values, scores = refs
    tiles, tok, size = queries.shape
    slots = past.shape[0] + 1
    members = min(GROUP, tiles)

    def block_of(slot):
        return now[...] if slot == 0 else past[table[slot - 1]]

    for slot in range(slots):
        values[:size, slot * tok : (slot + 1) * tok] = block_of(slot)[:, size:].T
    values[size:, :] = jnp.ones((LSE_ROWS, slots * tok), jnp.bfloat16)
    row_ids = lax.broadcasted_iota(jnp.int32, (LSE_ROWS, tok), 0)
    if merge:
        half = tiles // 2
        start = table[slots - 1]
        out_ref[pl.ds(start, half)] = near_part[...]
        out_ref[pl.ds(half - start, half)] = far_part[...]

    def one_group(group, _):
        base = slots + group * (3 * members)
        group_tiles = [table[base + member * 3] for member in range(members)]
        places = [table[base + member * 3 + 1] for member in range(members)]
        limits = [table[base + member * 3 + 2] for member in range(members)]
        most = functools.reduce(jnp.maximum, limits)

        if not merge:

            @pl.when(most == 0)
            def _():
                for tile in group_tiles:
                    out_ref[tile, :size, :] = jnp.zeros((size, tok), jnp.bfloat16)
                    out_ref[tile, size:, :] = jnp.where(row_ids == 0, NEG, 0.0).astype(jnp.bfloat16)

        def work(count):
            lanes = jnp.concatenate([queries[place].T for place in places], 1)
            peaks = [jnp.full((8, tok), NEG, jnp.float32) for _ in range(members)]
            for slot in range(count):
                raw = jnp.dot(block_of(slot)[:, :size], lanes, preferred_element_type=jnp.float32)
                scores[slot * tok : (slot + 1) * tok, :] = raw
                for member in range(members):
                    best = jnp.max(
                        raw[:, member * tok : (member + 1) * tok].reshape(tok // 8, 8, tok), axis=0
                    )
                    best = jnp.where(slot < limits[member], best, NEG)
                    peaks[member] = jnp.maximum(peaks[member], best)
            peaks = [jnp.max(peak, axis=0, keepdims=True) for peak in peaks]
            summed = None
            for low_slot in range(0, count, 2):
                chunk = []
                for slot in range(low_slot, min(low_slot + 2, count)):
                    shift = jnp.concatenate(
                        [jnp.where(slot < limits[member], peaks[member], -NEG) for member in range(members)], 1
                    )
                    chunk.append(
                        jnp.exp2(
                            (scores[slot * tok : (slot + 1) * tok, :] - shift) * (scale * math.log2(math.e))
                        ).astype(jnp.bfloat16)
                    )
                term = jnp.dot(
                    values[:, low_slot * tok : (low_slot + len(chunk)) * tok],
                    jnp.concatenate(chunk, 0),
                    preferred_element_type=jnp.float32,
                )
                summed = term if summed is None else summed + term
            total = jnp.maximum(summed[size : size + 1, :], 1.0)
            share = summed[:size, :] / total
            lse = jnp.concatenate(peaks, 1) * scale + jnp.log(total)
            if merge:
                others = [out_ref[tile] for tile in group_tiles]
                other_lse = jnp.concatenate(
                    [jnp.sum(other[size:, :].astype(jnp.float32), axis=0, keepdims=True) for other in others], 1
                )
                other_share = jnp.concatenate([other[:size, :] for other in others], 1).astype(jnp.float32)
                top = jnp.maximum(lse, other_lse)
                mine, theirs = jnp.exp(lse - top), jnp.exp(other_lse - top)
                both = mine + theirs
                share = share * (mine / both) + other_share * (theirs / both)
                lse = top + jnp.log(both)
            share = share.astype(jnp.bfloat16)
            high = lse.astype(jnp.bfloat16).astype(jnp.float32)
            rest = lse - high
            middle = rest.astype(jnp.bfloat16).astype(jnp.float32)
            low_part = rest - middle
            for member, tile in enumerate(group_tiles):
                cut = slice(member * tok, (member + 1) * tok)
                rows = jnp.where(row_ids == 0, high[:, cut], 0.0)
                rows = jnp.where(row_ids == 1, middle[:, cut], rows)
                rows = jnp.where(row_ids == 2, low_part[:, cut], rows)
                out_ref[tile, :size, :] = share[:, cut]
                out_ref[tile, size:, :] = rows.astype(jnp.bfloat16)

        low = 0
        for count in slot_buckets(slots):
            pl.when((most > low) & (most <= count))(functools.partial(work, count))
            low = count
        return 0

    lax.fori_loop(0, tiles // members, one_group, 0)


def attend_call(scale, table, queries, past, now, parts=()):
    tiles, tok, size = queries.shape
    slots = past.shape[0] + 1
    vmem = pl.BlockSpec(memory_space=pltpu.VMEM)
    return pl.pallas_call(
        functools.partial(attend_kernel, scale, bool(parts)),
        out_shape=jax.ShapeDtypeStruct((tiles, size + LSE_ROWS, tok), jnp.bfloat16),
        in_specs=[pl.BlockSpec(memory_space=pltpu.SMEM)] + [vmem] * (3 + len(parts)),
        out_specs=vmem,
        scratch_shapes=[
            pltpu.VMEM((size + LSE_ROWS, slots * tok), jnp.bfloat16),
            pltpu.VMEM((slots * tok, min(GROUP, tiles) * tok), jnp.float32),
        ],
        compiler_params=pltpu.CompilerParams(vmem_limit_bytes=32 * 2**20),
        cost_estimate=pl.CostEstimate(
            flops=10**6 * tiles, bytes_accessed=10**5, transcendentals=10**3 * tiles
        ),
        name="attend_last" if parts else "attend",
    )(table, queries, past, now, *parts)


def combine_kernel(in_ref, out_ref):
    tiles = in_ref.shape[0]
    tok, size = out_ref.shape
    lse = jnp.concatenate(
        [
            jnp.sum(in_ref[tile, size:, :].astype(jnp.float32), axis=0, keepdims=True)
            for tile in range(tiles)
        ],
        0,
    )
    factor = jnp.exp(lse - jnp.max(lse, axis=0, keepdims=True))
    factor = factor / jnp.sum(factor, axis=0, keepdims=True)
    total = in_ref[0, :size, :].astype(jnp.float32) * factor[0:1]
    for tile in range(1, tiles):
        total += in_ref[tile, :size, :].astype(jnp.float32) * factor[tile : tile + 1]
    out_ref[...] = total.T.astype(jnp.bfloat16)


def gather_bits(tiles):
    bits = [1 << k for k in range(tiles.bit_length() - 1)]
    return bits[-2::-1] + bits[-1:]


def ordered_table(by_rank, start, tile_ids, places, slots):
    count = slots.shape[0]
    ids = jnp.arange(count, dtype=jnp.int32)
    before = (slots[None, :] > slots[:, None]) | ((slots[None, :] == slots[:, None]) & (ids[None, :] < ids[:, None]))
    rank = jnp.sum(before.astype(jnp.int32), axis=1)
    chosen = rank[None, :] == ids[:, None]
    columns = jnp.stack([tile_ids, places, slots], 1)
    ordered = jnp.sum(jnp.where(chosen[:, :, None], columns[None], 0), axis=1)
    return jnp.concatenate([by_rank, start.reshape(1), ordered.reshape(-1)]).astype(jnp.int32)


def work_tables(frame_rank, frame_depth, tile_lists, position, core, tiles, frames):
    half_tiles = tiles // 2
    ids = jnp.arange(frames, dtype=jnp.int32)
    by_rank = jnp.sum(jnp.where(frame_rank[None, :] == (frames - 1 - ids)[:, None], ids[None, :], 0), axis=1)
    own = 2 * position + core
    mine = lax.dynamic_index_in_dim(tile_lists.reshape(tiles, 2, 2 * tiles), core, 1, False)
    depth = lax.dynamic_index_in_dim(frame_depth.reshape(tiles, 2), core, 1, False) + 1

    def slots_of(key_tile):
        return jnp.where(lax.dynamic_index_in_dim(mine, key_tile, 1, False) == 1, depth, 0)

    own_slots, other_slots = slots_of(own), slots_of(own + 1 - 2 * core)
    tile_ids = jnp.arange(tiles, dtype=jnp.int32)
    apart = tile_ids ^ position
    places = jnp.zeros_like(tile_ids)
    for k, bit in enumerate(gather_bits(tiles)):
        places = places + jnp.where((apart & bit) != 0, 1 << k, 0)
    start = position // half_tiles * half_tiles
    tables = []
    for first in (start, half_tiles - start):
        part_slots = lax.dynamic_slice_in_dim(own_slots, first, half_tiles)
        part_places = lax.dynamic_slice_in_dim(places, first, half_tiles) % half_tiles
        tables.append(ordered_table(by_rank, start, tile_ids[:half_tiles], part_places, part_slots))
    return tables + [ordered_table(by_rank, start, tile_ids, places, other_slots)]


def body(qkv_now, past_cache, frame_rank, frame_depth, tile_lists):
    tok = qkv_now.shape[0]
    size = qkv_now.shape[2] // 3
    space = lax.axis_size("space")
    frames = lax.axis_size("frame")
    tiles = space // 2
    index = lax.axis_index("space")
    position, core = index // 2, index % 2
    scale = 1.0 / math.sqrt(size)

    def swap(array, bit):
        return lax.ppermute(array, "space", [(i, i ^ bit) for i in range(space)])

    by_head = past_cache[0].transpose(1, 0, 2)
    by_head, qkv_now = lax.optimization_barrier((by_head, qkv_now))
    past_own = lax.all_to_all(by_head, "frame", split_axis=0, concat_axis=0, tiled=True)

    now = qkv_now[:, 0, :]
    near = now[None, :, :size]
    *bits, last_bit = gather_bits(tiles)
    for step, bit in enumerate(bits):
        near = jnp.concatenate([near, swap(near, 2 * bit)], 0)
        if step == 1:
            near, frame_rank, frame_depth, tile_lists = lax.optimization_barrier(
                (near, frame_rank, frame_depth, tile_lists)
            )
    now_own = now[:, size:]
    now_other = swap(now_own, 1)
    tables = work_tables(frame_rank, frame_depth, tile_lists, position, core, tiles, frames)

    far = swap(near, 2 * last_bit)
    near_part = attend_call(scale, tables[0], near, past_own, now_own)
    past_own, far, near_part, now_other = lax.optimization_barrier((past_own, far, near_part, now_other))
    past_other = swap(past_own, 1)
    far_part = attend_call(scale, tables[1], far, past_own, now_own)
    queries = jnp.concatenate([near, far], 0)
    partial = attend_call(scale, tables[2], queries, past_other, now_other, (near_part, far_part))
    groups = [[2 * place + which for place in range(tiles)] for which in range(2)]
    received = lax.all_to_all(
        partial, "space", split_axis=0, concat_axis=0, axis_index_groups=groups, tiled=True
    )
    return pl.pallas_call(
        combine_kernel,
        out_shape=jax.ShapeDtypeStruct((tok, size), jnp.bfloat16),
        compiler_params=pltpu.CompilerParams(vmem_limit_bytes=8 * 2**20),
        name="combine",
    )(received)


def solution(mesh):
    in_specs = (P("space", "frame", None), P("frame", "space", None, None), P(), P(), P())
    out_specs = P("space", "frame")
    return jax.shard_map(body, mesh=mesh, in_specs=in_specs, out_specs=out_specs, check_vma=False)
```

```python
import functools
import math

import jax
import jax.numpy as jnp
from jax import lax
from jax.experimental import pallas as pl
from jax.experimental.pallas import tpu as pltpu
from jax.sharding import PartitionSpec as P

NEG = -1e30
LSE_ROWS = 16
GROUP = 4


def slot_buckets(slots):
    sizes = [size for size in (1, 2, 3, 4, 5, 6, 7, 8, 9, 11, 13, 15) if size < slots]
    return sizes + [slots]


def attend_kernel(scale, merge, *refs):
    if merge:
        table, queries, past, now, near_part, far_part, out_ref, values, scores = refs
    else:
        table, queries, past, now, out_ref, values, scores = refs
    tiles, tok, size = queries.shape
    slots = past.shape[0] + 1
    members = min(GROUP, tiles)

    def block_of(slot):
        return now[...] if slot == 0 else past[table[slot - 1]]

    for slot in range(slots):
        values[:size, slot * tok : (slot + 1) * tok] = block_of(slot)[:, size:].T
    values[size:, :] = jnp.ones((LSE_ROWS, slots * tok), jnp.bfloat16)
    row_ids = lax.broadcasted_iota(jnp.int32, (LSE_ROWS, tok), 0)
    if merge:
        half = tiles // 2
        start = table[slots - 1]
        out_ref[pl.ds(start, half)] = near_part[...]
        out_ref[pl.ds(half - start, half)] = far_part[...]

    def one_group(group, _):
        base = slots + group * (3 * members)
        group_tiles = [table[base + member * 3] for member in range(members)]
        places = [table[base + member * 3 + 1] for member in range(members)]
        limits = [table[base + member * 3 + 2] for member in range(members)]
        most = functools.reduce(jnp.maximum, limits)

        if not merge:

            @pl.when(most == 0)
            def _():
                for tile in group_tiles:
                    out_ref[tile, :size, :] = jnp.zeros((size, tok), jnp.bfloat16)
                    out_ref[tile, size:, :] = jnp.where(row_ids == 0, NEG, 0.0).astype(jnp.bfloat16)

        def work(count):
            lanes = jnp.concatenate([queries[place].T for place in places], 1)
            peaks = [jnp.full((8, tok), NEG, jnp.float32) for _ in range(members)]
            for slot in range(count):
                raw = jnp.dot(block_of(slot)[:, :size], lanes, preferred_element_type=jnp.float32)
                scores[slot * tok : (slot + 1) * tok, :] = raw
                for member in range(members):
                    best = jnp.max(
                        raw[:, member * tok : (member + 1) * tok].reshape(tok // 8, 8, tok), axis=0
                    )
                    best = jnp.where(slot < limits[member], best, NEG)
                    peaks[member] = jnp.maximum(peaks[member], best)
            peaks = [jnp.max(peak, axis=0, keepdims=True) for peak in peaks]
            summed = None
            for low_slot in range(0, count, 2):
                chunk = []
                for slot in range(low_slot, min(low_slot + 2, count)):
                    shift = jnp.concatenate(
                        [jnp.where(slot < limits[member], peaks[member], -NEG) for member in range(members)], 1
                    )
                    chunk.append(
                        jnp.exp2(
                            (scores[slot * tok : (slot + 1) * tok, :] - shift) * (scale * math.log2(math.e))
                        ).astype(jnp.bfloat16)
                    )
                term = jnp.dot(
                    values[:, low_slot * tok : (low_slot + len(chunk)) * tok],
                    jnp.concatenate(chunk, 0),
                    preferred_element_type=jnp.float32,
                )
                summed = term if summed is None else summed + term
            total = jnp.maximum(summed[size : size + 1, :], 1.0)
            share = summed[:size, :] / total
            lse = jnp.concatenate(peaks, 1) * scale + jnp.log(total)
            if merge:
                others = [out_ref[tile] for tile in group_tiles]
                other_lse = jnp.concatenate(
                    [jnp.sum(other[size:, :].astype(jnp.float32), axis=0, keepdims=True) for other in others], 1
                )
                other_share = jnp.concatenate([other[:size, :] for other in others], 1).astype(jnp.float32)
                top = jnp.maximum(lse, other_lse)
                mine, theirs = jnp.exp(lse - top), jnp.exp(other_lse - top)
                both = mine + theirs
                share = share * (mine / both) + other_share * (theirs / both)
                lse = top + jnp.log(both)
            share = share.astype(jnp.bfloat16)
            high = lse.astype(jnp.bfloat16).astype(jnp.float32)
            rest = lse - high
            middle = rest.astype(jnp.bfloat16).astype(jnp.float32)
            low_part = rest - middle
            for member, tile in enumerate(group_tiles):
                cut = slice(member * tok, (member + 1) * tok)
                rows = jnp.where(row_ids == 0, high[:, cut], 0.0)
                rows = jnp.where(row_ids == 1, middle[:, cut], rows)
                rows = jnp.where(row_ids == 2, low_part[:, cut], rows)
                out_ref[tile, :size, :] = share[:, cut]
                out_ref[tile, size:, :] = rows.astype(jnp.bfloat16)

        low = 0
        for count in slot_buckets(slots):
            pl.when((most > low) & (most <= count))(functools.partial(work, count))
            low = count
        return 0

    lax.fori_loop(0, tiles // members, one_group, 0)


def attend_call(scale, table, queries, past, now, parts=()):
    tiles, tok, size = queries.shape
    slots = past.shape[0] + 1
    vmem = pl.BlockSpec(memory_space=pltpu.VMEM)
    return pl.pallas_call(
        functools.partial(attend_kernel, scale, bool(parts)),
        out_shape=jax.ShapeDtypeStruct((tiles, size + LSE_ROWS, tok), jnp.bfloat16),
        in_specs=[pl.BlockSpec(memory_space=pltpu.SMEM)] + [vmem] * (3 + len(parts)),
        out_specs=vmem,
        scratch_shapes=[
            pltpu.VMEM((size + LSE_ROWS, slots * tok), jnp.bfloat16),
            pltpu.VMEM((slots * tok, min(GROUP, tiles) * tok), jnp.float32),
        ],
        compiler_params=pltpu.CompilerParams(vmem_limit_bytes=32 * 2**20),
        cost_estimate=pl.CostEstimate(
            flops=10**6 * tiles, bytes_accessed=10**5, transcendentals=10**3 * tiles
        ),
        name="attend_last" if parts else "attend",
    )(table, queries, past, now, *parts)


def combine_kernel(in_ref, out_ref):
    tiles = in_ref.shape[0]
    tok, size = out_ref.shape
    lse = jnp.concatenate(
        [
            jnp.sum(in_ref[tile, size:, :].astype(jnp.float32), axis=0, keepdims=True)
            for tile in range(tiles)
        ],
        0,
    )
    factor = jnp.exp(lse - jnp.max(lse, axis=0, keepdims=True))
    factor = factor / jnp.sum(factor, axis=0, keepdims=True)
    total = in_ref[0, :size, :].astype(jnp.float32) * factor[0:1]
    for tile in range(1, tiles):
        total += in_ref[tile, :size, :].astype(jnp.float32) * factor[tile : tile + 1]
    out_ref[...] = total.T.astype(jnp.bfloat16)


def gather_bits(tiles):
    bits = [1 << k for k in range(tiles.bit_length() - 1)]
    return bits[-2::-1] + bits[-1:]


def ordered_table(by_rank, start, tile_ids, places, slots):
    count = slots.shape[0]
    ids = jnp.arange(count, dtype=jnp.int32)
    before = (slots[None, :] > slots[:, None]) | ((slots[None, :] == slots[:, None]) & (ids[None, :] < ids[:, None]))
    rank = jnp.sum(before.astype(jnp.int32), axis=1)
    chosen = rank[None, :] == ids[:, None]
    columns = jnp.stack([tile_ids, places, slots], 1)
    ordered = jnp.sum(jnp.where(chosen[:, :, None], columns[None], 0), axis=1)
    return jnp.concatenate([by_rank, start.reshape(1), ordered.reshape(-1)]).astype(jnp.int32)


def visible_slots(frame_rank, frame_depth, tile_lists, position, core, tiles, frames):
    ids = jnp.arange(frames, dtype=jnp.int32)
    by_rank = jnp.sum(jnp.where(frame_rank[None, :] == (frames - 1 - ids)[:, None], ids[None, :], 0), axis=1)
    own = 2 * position + core
    mine = lax.dynamic_index_in_dim(tile_lists.reshape(tiles, 2, 2 * tiles), core, 1, False)
    depth = lax.dynamic_index_in_dim(frame_depth.reshape(tiles, 2), core, 1, False) + 1

    def slots_of(key_tile):
        return jnp.where(lax.dynamic_index_in_dim(mine, key_tile, 1, False) == 1, depth, 0)

    return by_rank, slots_of(own), slots_of(own + 1 - 2 * core)


def work_tables(by_rank, own_slots, other_slots, position):
    tiles = own_slots.shape[0]
    half_tiles = tiles // 2
    tile_ids = jnp.arange(tiles, dtype=jnp.int32)
    apart = tile_ids ^ position
    places = jnp.zeros_like(tile_ids)
    for k, bit in enumerate(gather_bits(tiles)):
        places = places + jnp.where((apart & bit) != 0, 1 << k, 0)
    start = position // half_tiles * half_tiles
    tables = []
    for first in (start, half_tiles - start):
        part_slots = lax.dynamic_slice_in_dim(own_slots, first, half_tiles)
        part_places = lax.dynamic_slice_in_dim(places, first, half_tiles) % half_tiles
        tables.append(ordered_table(by_rank, start, tile_ids[:half_tiles], part_places, part_slots))
    return tables + [ordered_table(by_rank, start, tile_ids, places, other_slots)]


def body(qkv_now, past_cache, frame_rank, frame_depth, tile_lists):
    tok = qkv_now.shape[0]
    size = qkv_now.shape[2] // 3
    space = lax.axis_size("space")
    frames = lax.axis_size("frame")
    tiles = space // 2
    index = lax.axis_index("space")
    position, core = index // 2, index % 2
    scale = 1.0 / math.sqrt(size)

    def swap(array, bit):
        return lax.ppermute(array, "space", [(i, i ^ bit) for i in range(space)])

    by_head = past_cache[0].transpose(1, 0, 2)
    by_head, qkv_now = lax.optimization_barrier((by_head, qkv_now))
    past_own = lax.all_to_all(by_head, "frame", split_axis=0, concat_axis=0, tiled=True)

    now = qkv_now[:, 0, :]
    near = now[None, :, :size]
    slots = visible_slots(frame_rank, frame_depth, tile_lists, position, core, tiles, frames)
    *bits, last_bit = gather_bits(tiles)
    for step, bit in enumerate(bits):
        near = jnp.concatenate([near, swap(near, 2 * bit)], 0)
        if step == 1:
            near, slots = lax.optimization_barrier((near, slots))
    now_own = now[:, size:]
    now_other = swap(now_own, 1)
    tables = work_tables(*slots, position)

    far = swap(near, 2 * last_bit)
    near_part = attend_call(scale, tables[0], near, past_own, now_own)
    past_own, far, near_part, now_other = lax.optimization_barrier((past_own, far, near_part, now_other))
    past_other = swap(past_own, 1)
    far_part = attend_call(scale, tables[1], far, past_own, now_own)
    queries = jnp.concatenate([near, far], 0)
    partial = attend_call(scale, tables[2], queries, past_other, now_other, (near_part, far_part))
    groups = [[2 * place + which for place in range(tiles)] for which in range(2)]
    received = lax.all_to_all(
        partial, "space", split_axis=0, concat_axis=0, axis_index_groups=groups, tiled=True
    )
    return pl.pallas_call(
        combine_kernel,
        out_shape=jax.ShapeDtypeStruct((tok, size), jnp.bfloat16),
        compiler_params=pltpu.CompilerParams(vmem_limit_bytes=8 * 2**20),
        name="combine",
    )(received)


def solution(mesh):
    in_specs = (P("space", "frame", None), P("frame", "space", None, None), P(), P(), P())
    out_specs = P("space", "frame")
    return jax.shard_map(body, mesh=mesh, in_specs=in_specs, out_specs=out_specs, check_vma=False)
```
